256 devices in a mesh: fsdp: 8 (over z_lo, core), seq: 32 (over y, z_hi, x).
Axes of the slice: x: 4, y: 4, z: 8 (z_hi: 2, z_lo: 4; z = z_hi * 4 + z_lo), core: 2. Of those that a mesh axis runs over, the one named last changes fastest.
Arguments:
- query_tiles: bfloat16 [55296, 3072], P('seq', 'fsdp'), may hold values from -50 to 50
- key_tiles: bfloat16 [55296, 3072], P('seq', 'fsdp'), may hold values from -50 to 50
- value_tiles: bfloat16 [55296, 3072], P('seq', 'fsdp'), may hold values from -6 to 6
- slab_counts: int32 [32], P('seq'), may hold values from 1 to 3, 64 in all
- out_weight: bfloat16 [3072, 5120], P('seq', 'fsdp'), may hold values from -1.5 to 1.5
- out_bias: float32 [5120], P('fsdp'), may hold values from -3 to 3
Outputs:
- block_out: bfloat16 [5120, 55296], P('fsdp', 'seq')
The draws below stay inside these ranges and needn't reach their ends.
Inputs may be any that keep to these rules, and one draw needn't show every extreme that they name: slab_counts[d] is the number of consecutive tile frames held by device d of seq; they sum to 64, and some device holds 3.
All inputs are finite; a program needn't handle non-finite values.
Results may differ from the reference program's by a relative error of at most 0.024.
Values may be sent and summed in bfloat16 or wider, within the bound.
No kernel may reach another device: no remote copies, remote signals or barrier semaphores. Data moves between devices by JAX's collectives and lax.ppermute only.
A program may use at most 128 MiB of HBM per device.

```python
import math
import jax
import jax.numpy as jnp
import numpy as np
from jax import lax

D = 5120
HEADS = 24
HEAD = 128
TILE_TOK = 192
CAP = 3
FRAME = 576
HD = 3072
ROWS_CLIP = 55296
FRAMES_CLIP = 64
N_FSDP = 8
N_SEQ = 32


def draw_query_tiles(key, part):
    key = jax.random.fold_in(key, 3)
    shape = (N_SEQ * CAP, FRAME, HEADS, HEAD)
    drawn = jnp.clip(jax.random.normal(key, shape, jnp.float32), -4.0, 4.0)
    return drawn.reshape(N_SEQ * CAP * FRAME, HEADS * HEAD).astype(jnp.bfloat16)


def draw_key_tiles(key, part):
    key = jax.random.fold_in(key, 5)
    shape = (N_SEQ * CAP, FRAME, HEADS, HEAD)
    drawn = jnp.clip(jax.random.normal(key, shape, jnp.float32), -4.0, 4.0)
    return drawn.reshape(N_SEQ * CAP * FRAME, HEADS * HEAD).astype(jnp.bfloat16)


def steps_of(key, extent, pieces, low, top_value):
    gain, own = 1.0, jax.random.fold_in(key, 6)
    for axis_at, shards_of in pieces:
        steps = jnp.exp(jax.random.uniform(jax.random.fold_in(own, axis_at), (shards_of,), jnp.float32, low / len(pieces), top_value / len(pieces)))
        gain = gain * jnp.repeat(steps, extent[axis_at] // shards_of).reshape([-1 if axis == axis_at else 1 for axis in range(len(extent))])
    return gain


def profile(number_of, total, reach, slope):
    portions = [(1 << 20) // math.isqrt(standing ** slope) + 1 for standing in range(2, number_of + 1)]
    surplus, holding = total - reach - (number_of - 1), [1] * (number_of - 1)
    while surplus > 0:
        free = [i for i in range(number_of - 1) if holding[i] < reach]
        whole, budget = sum([portions[i] for i in free]), surplus
        for i in free:
            extra = min(reach - holding[i], max(1, budget * portions[i] // whole), surplus)
            holding[i] = holding[i] + extra
            surplus = surplus - extra
    return np.array([reach] + holding)


def ragged_sizes(key, number_of, total, bound, skew):
    if number_of == 2:
        one = jax.random.randint(key, (), max(1, total - bound), min(bound, total - 1) + 1)
        return jnp.stack([one, total - one])
    tallies = jnp.asarray(profile(number_of, total, bound, skew), jnp.int32)
    couples = (number_of - 1) // 2
    giver, sink = tallies[1:1 + 2 * couples:2], tallies[2:2 + 2 * couples:2]
    slack = jnp.minimum(giver - 1, bound - sink)
    shifted = jax.random.randint(jax.random.fold_in(key, 1), (couples,), 0, 1 << 20) % (slack + 1)
    tallies = tallies.at[1:1 + 2 * couples:2].set(giver - shifted).at[2:2 + 2 * couples:2].set(sink + shifted)
    return tallies[jax.random.permutation(jax.random.fold_in(key, 2), number_of)]


def centred(stream_key, extent, width, bound, pieces=(), kind=jnp.bfloat16):
    gain = steps_of(stream_key, extent, pieces, -0.22, 0.18) if pieces else 1.0
    result = jax.random.normal(stream_key, extent, jnp.float32) * width * gain
    return jnp.minimum(jnp.maximum(result, -bound), bound).astype(kind)


def setup_inputs(seed: int = 0) -> dict:
    seeds = jax.random.split(jax.random.key(seed), 7)
    return {
        "query_tiles": draw_query_tiles(jax.random.fold_in(seeds[6], 71), 0),
        "key_tiles": draw_key_tiles(jax.random.fold_in(seeds[6], 71), 0),
        "value_tiles": centred(seeds[2], (ROWS_CLIP, HD), 1.0, 6.0, ((0, 32), (1, 8))),
        "slab_counts": ragged_sizes(seeds[3], N_SEQ, 2 * N_SEQ, CAP, 2).astype(jnp.int32),
        "out_weight": centred(seeds[4], (HD, D), 16 ** -0.5, 1.5, ((0, 32), (1, 8))),
        "out_bias": centred(seeds[5], (D,), 0.5, 3.0, ((0, 8),), jnp.float32),
    }


def tile_near(frame_rows):
    query_tile = jnp.arange(frame_rows, dtype=jnp.int32) // TILE_TOK
    key_tile = (jnp.arange(3 * frame_rows, dtype=jnp.int32) % frame_rows) // TILE_TOK
    return jnp.abs(query_tile[:, None] - key_tile[None, :]) <= 1


def shifted_window(tiles):
    blank = jnp.zeros((1,) + tiles.shape[1:], tiles.dtype)
    padded = jnp.concatenate([blank, tiles, blank], axis=0)
    return jnp.concatenate([padded[:-2], padded[1:-1], padded[2:]], axis=1)


def reference(query_tiles, key_tiles, value_tiles, slab_counts, out_weight, out_bias):
    slot_total = N_SEQ * CAP
    counts = slab_counts.astype(jnp.int32)
    starts = (jnp.cumsum(counts) - counts).astype(jnp.int32)
    slot_index = jnp.arange(CAP, dtype=jnp.int32)
    frame_ids = (starts[:, None] + slot_index[None, :]).reshape(-1).astype(jnp.int32)
    occupied = (slot_index[None, :] < counts[:, None]).reshape(-1)
    target = jnp.where(occupied, frame_ids, FRAMES_CLIP).astype(jnp.int32)

    def compact(tiles):
        slots = tiles.reshape(slot_total, FRAME, HEADS, HEAD)
        holder = jnp.zeros((FRAMES_CLIP + 1, FRAME, HEADS, HEAD), tiles.dtype)
        return holder.at[target].set(slots)[:FRAMES_CLIP]

    query_frames = compact(query_tiles)
    key_set = shifted_window(compact(key_tiles))
    value_set = shifted_window(compact(value_tiles))
    order_ids = jnp.arange(FRAMES_CLIP, dtype=jnp.int32)
    block_ids = jnp.arange(3 * FRAME, dtype=jnp.int32) // FRAME
    block_ok = ((block_ids[None, :] != 0) | (order_ids[:, None] > 0)) & ((block_ids[None, :] != 2) | (order_ids[:, None] < FRAMES_CLIP - 1))
    near = tile_near(FRAME)
    group_width = HD // N_FSDP

    def frame_out(item):
        query_frame, key_frame, value_frame, frame_ok = item
        scores = jnp.einsum("qhd,khd->hqk", query_frame.astype(jnp.float32), key_frame.astype(jnp.float32)) * (HEAD ** -0.5)
        allowed = frame_ok[None, None, :] & near[None]
        scores = jnp.where(allowed, scores, -1e30)
        highest = jnp.max(scores, axis=-1, keepdims=True)
        expo = jnp.exp(scores - highest)
        weights = (expo / jnp.sum(expo, axis=-1, keepdims=True)).astype(jnp.bfloat16)
        attended = jnp.einsum("hqk,khd->qhd", weights.astype(jnp.float32), value_frame.astype(jnp.float32)).astype(jnp.bfloat16)
        attended = attended.reshape(FRAME, HD)
        total = jnp.zeros((FRAME, D), jnp.float32)
        for group in range(N_FSDP):
            features = attended[:, group * group_width:(group + 1) * group_width]
            rows = out_weight[group * group_width:(group + 1) * group_width]
            partial_value = jnp.dot(features, rows, preferred_element_type=jnp.float32).astype(jnp.bfloat16)
            total = total + partial_value.astype(jnp.float32)
        return (total + out_bias[None, :]).astype(jnp.bfloat16).T

    projected = lax.map(frame_out, (query_frames, key_set, value_set, block_ok))
    picked = projected[jnp.clip(frame_ids, 0, FRAMES_CLIP - 1)]
    picked = jnp.where(occupied[:, None, None], picked, jnp.zeros_like(picked))
    return jnp.transpose(picked, (1, 0, 2)).reshape(D, slot_total * FRAME)
```

```python
import functools

import jax
import jax.numpy as jnp
from jax import lax
from jax.experimental import pallas as pl
from jax.experimental.pallas import tpu as pltpu
from jax.sharding import Mesh
from jax.sharding import PartitionSpec as P

HEAD = 128
TILE = 192
FRAME = 576
LN2 = 0.6931471805599453
SCALE = HEAD**-0.5 / LN2
FAR = 1e30
SEQ = ("y", "zh", "x")
FSDP = ("zl", "core")
VMEM = 48 * 1024 * 1024


def attend_body(halo_total, info, q_ref, k_ref, v_ref, *rest):
    halos, (o_ref, kbuf, vbuf) = rest[:halo_total], rest[-3:]
    slot, prev_from, next_from, prev_ok, next_ok, active = (info[i] for i in range(6))

    @pl.when(pl.program_id(0) == 0)
    def _():
        vbuf[:, HEAD:] = jnp.ones((3 * FRAME, HEAD), jnp.bfloat16)

    @pl.when(active == 0)
    def _():
        o_ref[...] = jnp.zeros_like(o_ref)

    def fill(place, source):
        rows = pl.ds(place * FRAME, FRAME)

        @pl.when(source < 3)
        def _():
            local = pl.ds(pl.multiple_of(jnp.clip(source, 0, 2) * FRAME, FRAME), FRAME)
            kbuf[rows, :] = k_ref[local, :]
            vbuf[rows, :HEAD] = v_ref[local, :]

        for i in range(len(halos)):

            @pl.when(source == 3 + i)
            def _():
                kbuf[rows, :] = halos[i][:FRAME, :]
                vbuf[rows, :HEAD] = halos[i][FRAME:, :]

    @pl.when(active == 1)
    def _():
        fill(0, prev_from)
        fill(1, slot)
        fill(2, next_from)
        off = [jnp.where(prev_ok == 1, 0.0, FAR), jnp.float32(0.0), jnp.where(next_ok == 1, 0.0, FAR)]
        for w in range(3):
            low, high = max(0, w - 1) * TILE, min(3, w + 2) * TILE
            q = q_ref[pl.ds(pl.multiple_of(slot * FRAME + w * TILE, TILE), TILE), :]
            scores, tops = [], []
            for f in range(3):
                keys = kbuf[f * FRAME + low : f * FRAME + high, :]
                s = lax.dot_general(q, keys, (((1,), (1,)), ((), ())), preferred_element_type=jnp.float32)
                scores.append(s)
                tops.append(jnp.max(s, axis=1, keepdims=True) * SCALE - off[f])
            top = jnp.maximum(jnp.maximum(tops[0], tops[1]), tops[2])
            total = None
            for f in range(3):
                p = jnp.exp2(scores[f] * SCALE - (top + off[f])).astype(jnp.bfloat16)
                part = jnp.dot(
                    p, vbuf[f * FRAME + low : f * FRAME + high, :], preferred_element_type=jnp.float32
                )
                total = part if total is None else total + part
            o_ref[w * TILE : (w + 1) * TILE, :] = (total[:, :HEAD] / total[:, HEAD:]).astype(jnp.bfloat16)


def attend(info, query, key, value, halos, after):
    rows, width = query.shape
    heads = width // HEAD
    column = lambda h, info: (0, h)
    whole = pl.BlockSpec((rows, HEAD), column)
    one = pl.BlockSpec((FRAME, HEAD), column)
    two = pl.BlockSpec((2 * FRAME, HEAD), column)
    return pl.pallas_call(
        functools.partial(attend_body, len(halos)),
        out_shape=jax.ShapeDtypeStruct((FRAME, width), jnp.bfloat16),
        grid_spec=pltpu.PrefetchScalarGridSpec(
            num_scalar_prefetch=1,
            grid=(heads,),
            in_specs=[whole] * 3 + [two] * len(halos) + [pl.BlockSpec(memory_space=pl.ANY)] * len(after),
            out_specs=one,
            scratch_shapes=[
                pltpu.VMEM((3 * FRAME, HEAD), jnp.bfloat16),
                pltpu.VMEM((3 * FRAME, 2 * HEAD), jnp.bfloat16),
            ],
        ),
        compiler_params=pltpu.CompilerParams(vmem_limit_bytes=VMEM),
        cost_estimate=pl.CostEstimate(flops=4 * 10**9, bytes_accessed=6 * 10**6, transcendentals=3 * 10**6),
    )(info, query, key, value, *halos, *after)


def project_body(info, x0, x1, x2, x3, w_ref, mine_ref, other_ref):
    total = None
    for k, x in enumerate((x0, x1, x2, x3)):
        width = x.shape[1]
        rows = pl.ds(pl.multiple_of(info[k] * width, width), width)
        part = jnp.dot(x[...], w_ref[rows, :], preferred_element_type=jnp.float32)
        total = part if total is None else total + part

    @pl.when(pl.program_id(0) == 0)
    def _():
        other_ref[...] = total.astype(jnp.bfloat16)

    @pl.when(pl.program_id(0) == 1)
    def _():
        mine_ref[...] = total


def project(order, pieces, weight):
    rows, width = pieces[0].shape
    depth, both = weight.shape
    columns = both // 2
    fixed = lambda j, info: (0, 0)
    return pl.pallas_call(
        project_body,
        out_shape=(
            jax.ShapeDtypeStruct((rows, columns), jnp.float32),
            jax.ShapeDtypeStruct((rows, columns), jnp.bfloat16),
        ),
        grid_spec=pltpu.PrefetchScalarGridSpec(
            num_scalar_prefetch=1,
            grid=(2,),
            in_specs=[pl.BlockSpec((rows, width), fixed)] * 4
            + [pl.BlockSpec((depth, columns), lambda j, info: (0, 1 - j))],
            out_specs=[pl.BlockSpec((rows, columns), fixed)] * 2,
        ),
        compiler_params=pltpu.CompilerParams(vmem_limit_bytes=VMEM),
        cost_estimate=pl.CostEstimate(
            flops=2 * rows * depth * both, bytes_accessed=2 * depth * (both + rows), transcendentals=0
        ),
    )(order, *pieces, weight)


def finish_body(info, mine_ref, received_ref, bias_ref, *rest):
    value = mine_ref[...] + received_ref[...].astype(jnp.float32) + bias_ref[...]
    rest[-1][...] = jnp.where(info[1] == 1, value, 0.0).astype(jnp.bfloat16)


def finish(info, mine, received, bias, out):
    rows, columns = mine.shape
    whole = pl.BlockSpec((rows, columns), lambda j, info: (0, 0))
    extra = [] if out is None else [out]
    return pl.pallas_call(
        finish_body,
        out_shape=jax.ShapeDtypeStruct((3 * rows, columns), jnp.bfloat16),
        grid_spec=pltpu.PrefetchScalarGridSpec(
            num_scalar_prefetch=1,
            grid=(1,),
            in_specs=[whole, whole, pl.BlockSpec((1, columns), lambda j, info: (0, 0))]
            + [pl.BlockSpec(memory_space=pl.ANY)] * len(extra),
            out_specs=pl.BlockSpec((rows, columns), lambda j, info: (info[0], 0)),
        ),
        input_output_aliases={4: 0} if extra else {},
        compiler_params=pltpu.CompilerParams(vmem_limit_bytes=VMEM),
    )(info, mine, received, bias.reshape(1, columns), *extra)


def lay_body(info, own_ref, beside_ref, across_ref, askew_ref, out_ref):
    columns = own_ref.shape[1]
    home = info[0] == 1
    out_ref[:, :columns] = jnp.where(home, own_ref[...], across_ref[...])
    out_ref[:, columns:] = jnp.where(home, beside_ref[...], askew_ref[...])


def lay(info, own, beside, across, askew):
    rows, columns = own.shape
    vmem = pl.BlockSpec(memory_space=pltpu.VMEM)
    return pl.pallas_call(
        lay_body,
        out_shape=jax.ShapeDtypeStruct((rows, 2 * columns), own.dtype),
        in_specs=[pl.BlockSpec(memory_space=pltpu.SMEM)] + [vmem] * 4,
        out_specs=vmem,
    )(info, own, beside, across, askew)


def on_device(query, key, value, slab_counts, out_weight, out_bias):
    count = slab_counts[0]
    x, zh, zl, core = (lax.axis_index(name) for name in ("x", "zh", "zl", "core"))
    seq = lax.axis_index(SEQ)
    seq_width = lax.axis_size(SEQ)
    even = x % 2 == 0
    last = count - 1

    near, away = [], []
    for s in range(seq_width):
        near.append((s, s + 1 if s % 2 == 0 else s - 1))
        t = s - 1 if s % 2 == 0 else s + 1
        if 0 <= t < seq_width:
            away.append((s, t))

    def frame_of(array, index):
        return lax.dynamic_slice_in_dim(array, index * FRAME, FRAME, 0)

    near_slot = jnp.where(even, last, 0)
    away_slot = jnp.where(even, 0, last)
    both = jnp.concatenate([frame_of(key, near_slot), frame_of(value, near_slot)], axis=0)
    near_halo = [lax.ppermute(both, SEQ, near)]
    both = jnp.concatenate([frame_of(key, away_slot), frame_of(value, away_slot)], axis=0)
    away_halo = [lax.ppermute(both, SEQ, away)]

    pair = ("core", "zh")
    beside = lax.ppermute(out_weight, pair, [(2, 0), (1, 3)])
    across = lax.ppermute(out_weight, pair, [(0, 1), (3, 2)])
    askew = lax.ppermute(out_weight, pair, [(2, 1), (1, 2)])
    near_end = jnp.where(even, last, 0)
    away_end = jnp.where(even, 0, last)
    slots = [
        jnp.where(count == 3, 1, jnp.where(count == 2, 2, 1)),
        jnp.where(count == 1, 2, near_end),
        jnp.where(count == 1, 0, away_end),
    ]
    actives = [count == 3, count >= 2, count >= 1]
    lines = lax.axis_size("zl")

    def along(value, steps):
        return lax.ppermute(value, "zl", [(i, (i + steps) % lines) for i in range(lines)])

    gathered = []
    for c, halos in enumerate(([], near_halo, near_halo + away_halo)):
        slot = slots[c]
        prev_from = jnp.where(slot > 0, slot - 1, jnp.where(even, 4, 3))
        next_from = jnp.where(slot < last, slot + 1, jnp.where(even, 3, 4))
        prev_ok = (slot > 0) | (seq > 0)
        next_ok = (slot < last) | (seq < seq_width - 1)
        info = jnp.stack(
            [v.astype(jnp.int32) for v in (slot, prev_from, next_from, prev_ok, next_ok, actives[c])]
        )
        chunk = attend(info, query, key, value, halos, [])
        ahead, behind = along(chunk, 1), along(chunk, -1)
        gathered.append([chunk, ahead, along(chunk, 2) if c == 0 else along(ahead, 1), behind])

    laid = lay((zh == core).astype(jnp.int32).reshape(1), out_weight, beside, across, askew)
    weight = lax.all_gather(laid, ("y", "x"), axis=0, tiled=True)
    order = jnp.stack([(zl - k) % lines for k in range(lines)]).astype(jnp.int32)
    out = None
    for slot, active, pieces in zip(slots, actives, gathered):
        own, other = project(order, pieces, weight)
        received = lax.ppermute(other, "core", [(0, 1), (1, 0)])
        info = jnp.stack([slot.astype(jnp.int32), active.astype(jnp.int32)])
        out = finish(info, own, received, out_bias, out)
    return out.T


def solution(mesh):
    fine = Mesh(mesh.devices.reshape(4, 2, 4, 2, 4), FSDP + SEQ)
    tiles = P(SEQ, FSDP)
    return jax.shard_map(
        on_device,
        mesh=fine,
        in_specs=(tiles, tiles, tiles, P(SEQ), tiles, P(FSDP)),
        out_specs=P(FSDP, SEQ),
        check_vma=False,
    )
```

```python
import functools

import jax
import jax.numpy as jnp
from jax import lax
from jax.experimental import pallas as pl
from jax.experimental.pallas import tpu as pltpu
from jax.sharding import Mesh
from jax.sharding import PartitionSpec as P

HEAD = 128
TILE = 192
FRAME = 576
LN2 = 0.6931471805599453
SCALE = HEAD**-0.5 / LN2
FAR = 1e30
SEQ = ("y", "zh", "x")
FSDP = ("zl", "core")
VMEM = 48 * 1024 * 1024
FREE = pl.CostEstimate(flops=0, bytes_accessed=0, transcendentals=0)


def attend_body(halo_total, info, q_ref, k_ref, v_ref, *rest):
    halos, (o_ref, kbuf, vbuf) = rest[:halo_total], rest[-3:]
    slot, prev_from, next_from, prev_ok, next_ok, active = (info[i] for i in range(6))

    @pl.when(pl.program_id(0) == 0)
    def _():
        vbuf[:, HEAD:] = jnp.ones((3 * FRAME, HEAD), jnp.bfloat16)

    @pl.when(active == 0)
    def _():
        o_ref[...] = jnp.zeros_like(o_ref)

    def fill(place, source):
        rows = pl.ds(place * FRAME, FRAME)

        @pl.when(source < 3)
        def _():
            local = pl.ds(pl.multiple_of(jnp.clip(source, 0, 2) * FRAME, FRAME), FRAME)
            kbuf[rows, :] = k_ref[local, :]
            vbuf[rows, :HEAD] = v_ref[local, :]

        for i in range(halo_total // 2):

            @pl.when(source == 3 + i)
            def _():
                kbuf[rows, :] = halos[2 * i][...]
                vbuf[rows, :HEAD] = halos[2 * i + 1][...]

    @pl.when(active == 1)
    def _():
        fill(0, prev_from)
        fill(1, slot)
        fill(2, next_from)
        off = [jnp.where(prev_ok == 1, 0.0, FAR), jnp.float32(0.0), jnp.where(next_ok == 1, 0.0, FAR)]
        for w in range(3):
            low, high = max(0, w - 1) * TILE, min(3, w + 2) * TILE
            q = q_ref[pl.ds(pl.multiple_of(slot * FRAME + w * TILE, TILE), TILE), :]
            scores, tops = [], []
            for f in range(3):
                keys = kbuf[f * FRAME + low : f * FRAME + high, :]
                s = lax.dot_general(q, keys, (((1,), (1,)), ((), ())), preferred_element_type=jnp.float32)
                scores.append(s)
                tops.append(jnp.max(s, axis=1, keepdims=True) * SCALE - off[f])
            top = jnp.maximum(jnp.maximum(tops[0], tops[1]), tops[2])
            total = None
            for f in range(3):
                p = jnp.exp2(scores[f] * SCALE - (top + off[f])).astype(jnp.bfloat16)
                part = jnp.dot(
                    p, vbuf[f * FRAME + low : f * FRAME + high, :], preferred_element_type=jnp.float32
                )
                total = part if total is None else total + part
            o_ref[w * TILE : (w + 1) * TILE, :] = (total[:, :HEAD] / total[:, HEAD:]).astype(jnp.bfloat16)


def attend(info, query, key, value, halos, after):
    rows, width = query.shape
    heads = width // HEAD
    column = lambda h, info: (0, h)
    whole = pl.BlockSpec((rows, HEAD), column)
    one = pl.BlockSpec((FRAME, HEAD), column)
    where = [pl.BlockSpec((FRAME, HEAD), lambda h, info, r=r: (r, h)) for _, r in halos]
    return pl.pallas_call(
        functools.partial(attend_body, len(halos)),
        out_shape=jax.ShapeDtypeStruct((FRAME, width), jnp.bfloat16),
        grid_spec=pltpu.PrefetchScalarGridSpec(
            num_scalar_prefetch=1,
            grid=(heads,),
            in_specs=[whole] * 3 + where + [pl.BlockSpec(memory_space=pl.ANY)] * len(after),
            out_specs=one,
            scratch_shapes=[
                pltpu.VMEM((3 * FRAME, HEAD), jnp.bfloat16),
                pltpu.VMEM((3 * FRAME, 2 * HEAD), jnp.bfloat16),
            ],
        ),
        compiler_params=pltpu.CompilerParams(vmem_limit_bytes=VMEM),
        cost_estimate=FREE,
    )(info, query, key, value, *[array for array, _ in halos], *after)


def share(info, at, pieces, w_ref):
    total = None
    for k, piece in enumerate(pieces):
        width = piece.shape[1]
        rows = pl.ds(pl.multiple_of(info[at + k] * width, width), width)
        part = jnp.dot(piece[...], w_ref[rows, :], preferred_element_type=jnp.float32)
        total = part if total is None else total + part
    return total


def hand_out(total, mine_ref, other_ref):
    @pl.when(pl.program_id(0) == 0)
    def _():
        other_ref[...] = total.astype(jnp.bfloat16)

    @pl.when(pl.program_id(0) == 1)
    def _():
        mine_ref[...] = total


def project_body(split, info, *refs):
    groups, at = [], 0
    for size in split:
        groups.append(refs[at : at + size])
        at += size
    w_ref, outs = refs[at], refs[at + 1 :]
    hand_out(share(info, 0, groups[0], w_ref), outs[0], outs[1])
    if len(groups) == 2:
        outs[2][...] = share(info, len(groups[0]), groups[1], w_ref)


def project_last_body(info, piece, w_ref, so_far, mine_ref, other_ref):
    hand_out(share(info, 1, [piece], w_ref) + so_far[...], mine_ref, other_ref)


def project(order, whole, part, weight, so_far=None):
    rows, width = whole[0].shape
    depth, both = weight.shape
    columns = both // 2
    fixed = lambda j, info: (0, 0)
    side = lambda j, info: (0, 1 - j)
    block = pl.BlockSpec((rows, columns), side)
    out_shape = [
        jax.ShapeDtypeStruct((rows, columns), jnp.float32),
        jax.ShapeDtypeStruct((rows, columns), jnp.bfloat16),
    ]
    out_specs = [pl.BlockSpec((rows, columns), fixed)] * 2
    in_specs = [pl.BlockSpec((rows, width), fixed)] * (len(whole) + len(part))
    if part:
        out_shape.append(jax.ShapeDtypeStruct((rows, both), jnp.float32))
        out_specs.append(block)
    if so_far is None:
        body, more = functools.partial(project_body, [len(g) for g in (whole, part) if g]), []
        in_specs.append(pl.BlockSpec((depth, columns), side))
    else:
        body, more = project_last_body, [so_far]
        in_specs += [pl.BlockSpec((width, columns), lambda j, info: (info[0], 1 - j)), block]
    return pl.pallas_call(
        body,
        out_shape=out_shape,
        grid_spec=pltpu.PrefetchScalarGridSpec(
            num_scalar_prefetch=1, grid=(2,), in_specs=in_specs, out_specs=out_specs
        ),
        compiler_params=pltpu.CompilerParams(vmem_limit_bytes=VMEM),
        cost_estimate=FREE,
    )(order, *whole, *part, weight, *more)


def finish_body(total, info, *refs):
    bias_ref, out_ref = refs[2 * total], refs[-1]
    for i in range(total):

        @pl.when(pl.program_id(0) == i)
        def _():
            value = refs[2 * i][...] + refs[2 * i + 1][...].astype(jnp.float32) + bias_ref[...]
            out_ref[...] = jnp.where(info[total + i] == 1, value, 0.0).astype(jnp.bfloat16)


def finish(info, parts, bias, out):
    rows, columns = parts[0].shape
    total = len(parts) // 2
    whole = pl.BlockSpec((rows, columns), lambda j, info: (0, 0))
    extra = [] if out is None else [out]
    return pl.pallas_call(
        functools.partial(finish_body, total),
        out_shape=jax.ShapeDtypeStruct((3 * rows, columns), jnp.bfloat16),
        grid_spec=pltpu.PrefetchScalarGridSpec(
            num_scalar_prefetch=1,
            grid=(total,),
            in_specs=[whole] * len(parts)
            + [pl.BlockSpec((1, columns), lambda j, info: (0, 0))]
            + [pl.BlockSpec(memory_space=pl.ANY)] * len(extra),
            out_specs=pl.BlockSpec((rows, columns), lambda j, info: (info[j], 0)),
        ),
        input_output_aliases={2 + len(parts): 0} if extra else {},
        compiler_params=pltpu.CompilerParams(vmem_limit_bytes=VMEM),
        cost_estimate=FREE,
    )(info, *parts, bias.reshape(1, columns), *extra)


def pack_body(info, k0_ref, v0_ref, k1_ref, v1_ref, near_ref, key_ref, value_ref):
    near_ref[:FRAME, :] = k0_ref[...]
    near_ref[FRAME:, :] = v0_ref[...]
    key_ref[...] = k1_ref[...]
    value_ref[...] = v1_ref[...]


def pack(info, key, value):
    width = key.shape[1]
    frames = [pl.BlockSpec((FRAME, width), lambda i, info, c=c: (info[c], 0)) for c in (0, 0, 1, 1)]
    heights = (2 * FRAME, FRAME, FRAME)
    return pl.pallas_call(
        pack_body,
        out_shape=[jax.ShapeDtypeStruct((rows, width), key.dtype) for rows in heights],
        grid_spec=pltpu.PrefetchScalarGridSpec(
            num_scalar_prefetch=1,
            grid=(1,),
            in_specs=frames,
            out_specs=[pl.BlockSpec((rows, width), lambda i, info: (0, 0)) for rows in heights],
        ),
        compiler_params=pltpu.CompilerParams(vmem_limit_bytes=VMEM),
        cost_estimate=FREE,
    )(info, key, value, key, value)


def lay_body(info, own_ref, beside_ref, across_ref, askew_ref, *rest):
    out_ref = rest[-1]
    columns = own_ref.shape[1]
    home = info[0] == 1
    out_ref[:, :columns] = jnp.where(home, own_ref[...], across_ref[...])
    out_ref[:, columns:] = jnp.where(home, beside_ref[...], askew_ref[...])


def lay(info, own, beside, across, askew, after):
    rows, columns = own.shape
    vmem = pl.BlockSpec(memory_space=pltpu.VMEM)
    return pl.pallas_call(
        lay_body,
        out_shape=jax.ShapeDtypeStruct((rows, 2 * columns), own.dtype),
        in_specs=[pl.BlockSpec(memory_space=pltpu.SMEM)] + [vmem] * 4
        + [pl.BlockSpec(memory_space=pl.ANY)] * len(after),
        out_specs=vmem,
        cost_estimate=FREE,
    )(info, own, beside, across, askew, *after)


def on_device(query, key, value, slab_counts, out_weight, out_bias):
    count = slab_counts[0]
    x, zh, zl, core = (lax.axis_index(name) for name in ("x", "zh", "zl", "core"))
    seq = lax.axis_index(SEQ)
    seq_width, row = lax.axis_size(SEQ), lax.axis_size("x")
    even = x % 2 == 0
    last = count - 1

    near_slot = jnp.where(even, last, 0)
    away_slot = jnp.where(even, 0, last)
    near_pack, away_key, away_value = pack(jnp.stack([near_slot, away_slot]), key, value)
    near = lax.ppermute(near_pack, "x", [(0, 1), (1, 0), (2, 3), (3, 2)])
    key_round = lax.ppermute(away_key, "x", [(0, 3), (3, 0), (1, 2), (2, 1)])
    value_side = lax.ppermute(away_value, "x", [(0, 1), (3, 2)])
    value_inner = lax.ppermute(away_value, "x", [(1, 2), (2, 1)])

    def across_rows(value, up, down):
        rows = range(seq_width // row - 1)
        pairs = [(r * row + up, (r + 1) * row + up) for r in rows]
        pairs += [((r + 1) * row + down, r * row + down) for r in rows]
        return lax.ppermute(value, SEQ, pairs)

    key_far = across_rows(key_round, 0, 3)
    value_far = lax.ppermute(across_rows(value_side, 2, 1), "x", [(2, 0), (1, 3)])
    near_halo = [(near, 0), (near, 1)]
    inner_halo = [(key_round, 0), (value_inner, 0)]
    far_halo = [(key_far, 0), (value_far, 0)]

    slots = [
        jnp.where(count == 3, 1, jnp.where(count == 2, 2, 1)),
        jnp.where(count == 1, 2, near_slot),
        jnp.where(count == 1, 0, away_slot),
    ]
    actives = [count == 3, count >= 2, count >= 1]
    away_from = jnp.where((x == 1) | (x == 2), 4, 5)

    def frame(c, halos, after):
        slot = slots[c]
        prev_from = jnp.where(slot > 0, slot - 1, jnp.where(even, away_from, 3))
        next_from = jnp.where(slot < last, slot + 1, jnp.where(even, 3, away_from))
        prev_ok = (slot > 0) | (seq > 0)
        next_ok = (slot < last) | (seq < seq_width - 1)
        info = jnp.stack(
            [v.astype(jnp.int32) for v in (slot, prev_from, next_from, prev_ok, next_ok, actives[c])]
        )
        return attend(info, query, key, value, halos, after)

    lines = lax.axis_size("zl")

    def along(value, steps):
        return lax.ppermute(value, "zl", [(i, (i + steps) % lines) for i in range(lines)])

    a = frame(0, [], [])
    a1, a3 = along(a, 1), along(a, -1)
    b = frame(1, near_halo, [])
    b1, b3 = along(b, 1), along(b, -1)
    c = frame(2, near_halo + inner_halo + far_halo, [a1, a3, b1, b3])
    a2, b2 = along(a1, 1), along(b1, 1)
    c1, c3 = along(c, 1), along(c, -1)
    c2 = along(c1, 1)

    pair = ("core", "zh")
    beside = lax.ppermute(out_weight, pair, [(2, 0), (1, 3)])
    across = lax.ppermute(out_weight, pair, [(0, 1), (3, 2)])
    askew = lax.ppermute(out_weight, pair, [(2, 1), (1, 2)])
    home = (zh == core).astype(jnp.int32).reshape(1)
    laid = lay(home, out_weight, beside, across, askew, [key_round, value_side, near, a1])
    weight = lax.all_gather(laid, ("y", "x"), axis=0, tiled=True)

    order = [((zl - k) % lines).astype(jnp.int32) for k in range(lines)]

    def swap(value):
        return lax.ppermute(value, "core", [(0, 1), (1, 0)])

    def put(indices, parts, out):
        info = jnp.stack([v[i].astype(jnp.int32) for v in (slots, actives) for i in indices])
        return finish(info, parts, out_bias, out)

    own_a, other_a = project(jnp.stack(order), [a, a1, a2, a3], [], weight)
    out = put([0], [own_a, swap(other_a)], None)
    turns = jnp.stack(order + [order[0], order[1], order[3]])
    own_b, other_b, so_far = project(turns, [b, b1, b2, b3], [c, c1, c3], weight)
    own_c, other_c = project(jnp.stack([order[2], jnp.zeros_like(order[2])]), [c2], [], weight, so_far)
    out = put([1, 2], [own_b, swap(other_b), own_c, swap(other_c)], out)
    return out.T


def solution(mesh):
    fine = Mesh(mesh.devices.reshape(4, 2, 4, 2, 4), FSDP + SEQ)
    tiles = P(SEQ, FSDP)
    return jax.shard_map(
        on_device,
        mesh=fine,
        in_specs=(tiles, tiles, tiles, P(SEQ), tiles, P(FSDP)),
        out_specs=P(FSDP, SEQ),
        check_vma=False,
    )
```

```python
import functools

import jax
import jax.numpy as jnp
from jax import lax
from jax.experimental import pallas as pl
from jax.experimental.pallas import tpu as pltpu
from jax.sharding import Mesh
from jax.sharding import PartitionSpec as P

HEAD = 128
TILE = 192
FRAME = 576
LN2 = 0.6931471805599453
SCALE = HEAD**-0.5 / LN2
FAR = 1e30
SEQ = ("y", "zh", "x")
FSDP = ("zl", "core")
VMEM = 48 * 1024 * 1024
FREE = pl.CostEstimate(flops=0, bytes_accessed=0, transcendentals=0)


def attend_body(halo_total, info, q_ref, k_ref, v_ref, *rest):
    halos, (o_ref, kbuf, vbuf) = rest[:halo_total], rest[-3:]
    slot, prev_from, next_from, prev_ok, next_ok, active = (info[i] for i in range(6))

    @pl.when(active == 0)
    def _():
        o_ref[...] = jnp.zeros_like(o_ref)

    def fill(place, source):
        rows = pl.ds(place * FRAME, FRAME)

        @pl.when(source < 3)
        def _():
            local = pl.ds(pl.multiple_of(jnp.clip(source, 0, 2) * FRAME, FRAME), FRAME)
            kbuf[rows, :] = k_ref[local, :]
            vbuf[rows, :] = v_ref[local, :]

        for i in range(halo_total // 2):

            @pl.when(source == 3 + i)
            def _():
                kbuf[rows, :] = halos[2 * i][...]
                vbuf[rows, :] = halos[2 * i + 1][...]

    @pl.when(active == 1)
    def _():
        fill(0, prev_from)
        fill(1, slot)
        fill(2, next_from)
        off = [jnp.where(prev_ok == 1, 0.0, FAR), jnp.float32(0.0), jnp.where(next_ok == 1, 0.0, FAR)]
        for w in range(3):
            low, high = max(0, w - 1) * TILE, min(3, w + 2) * TILE
            q = q_ref[pl.ds(pl.multiple_of(slot * FRAME + w * TILE, TILE), TILE), :]
            scores, tops = [], []
            for f in range(3):
                keys = kbuf[f * FRAME + low : f * FRAME + high, :]
                s = lax.dot_general(q, keys, (((1,), (1,)), ((), ())), preferred_element_type=jnp.float32)
                scores.append(s)
                tops.append(jnp.max(s, axis=1, keepdims=True) * SCALE - off[f])
            top = jnp.maximum(jnp.maximum(tops[0], tops[1]), tops[2])
            total, mass = None, None
            for f in range(3):
                p = jnp.exp2(scores[f] * SCALE - (top + off[f]))
                values = vbuf[f * FRAME + low : f * FRAME + high, :]
                part = jnp.dot(p.astype(jnp.bfloat16), values, preferred_element_type=jnp.float32)
                row = jnp.sum(p, axis=1, keepdims=True)
                total, mass = (part, row) if total is None else (total + part, mass + row)
            o_ref[w * TILE : (w + 1) * TILE, :] = (total / mass).astype(jnp.bfloat16)


def attend(info, query, key, value, halos, after):
    rows, width = query.shape
    heads = width // HEAD
    column = lambda h, info: (0, h)
    whole = pl.BlockSpec((rows, HEAD), column)
    one = pl.BlockSpec((FRAME, HEAD), column)
    where = [pl.BlockSpec((FRAME, HEAD), lambda h, info, r=r: (r, h)) for _, r in halos]
    return pl.pallas_call(
        functools.partial(attend_body, len(halos)),
        out_shape=jax.ShapeDtypeStruct((FRAME, width), jnp.bfloat16),
        grid_spec=pltpu.PrefetchScalarGridSpec(
            num_scalar_prefetch=1,
            grid=(heads,),
            in_specs=[whole] * 3 + where + [pl.BlockSpec(memory_space=pl.ANY)] * len(after),
            out_specs=one,
            scratch_shapes=[
                pltpu.VMEM((3 * FRAME, HEAD), jnp.bfloat16),
                pltpu.VMEM((3 * FRAME, HEAD), jnp.bfloat16),
            ],
        ),
        compiler_params=pltpu.CompilerParams(vmem_limit_bytes=VMEM),
        cost_estimate=FREE,
    )(info, query, key, value, *[array for array, _ in halos], *after)


def line_up(info, at, pieces, line):
    width = pieces[0].shape[1]
    if len(pieces) * width < line.shape[1]:
        line[...] = jnp.zeros_like(line)
    for k, piece in enumerate(pieces):
        line[:, pl.ds(pl.multiple_of(info[at + k] * width, width), width)] = piece[...]


def hand_out(total, mine_ref, other_ref):
    mine_ref[...] = total[:, :HEAD]
    other_ref[...] = total[:, HEAD:].astype(jnp.bfloat16)


def project_body(split, info, *refs):
    total = sum(split)
    w_ref, lines = refs[total], refs[len(refs) - len(split) :]
    outs = refs[total + 1 :]

    @pl.when(pl.program_id(0) == 0)
    def _():
        at = 0
        for size, line in zip(split, lines):
            line_up(info, at, refs[at : at + size], line)
            at += size

    hand_out(jnp.dot(lines[0][...], w_ref[...], preferred_element_type=jnp.float32), outs[0], outs[1])
    if len(split) == 2:
        outs[2][...] = jnp.dot(lines[1][...], w_ref[...], preferred_element_type=jnp.float32)


def project_last_body(info, piece, w_ref, so_far, mine_ref, other_ref):
    part = jnp.dot(piece[...], w_ref[...], preferred_element_type=jnp.float32)
    hand_out(part + so_far[...], mine_ref, other_ref)


def project(order, whole, part, weight, so_far=None):
    rows, width = whole[0].shape
    depth, both = weight.shape
    fixed = lambda j, info: (0, 0)
    side = lambda j, info: (0, j)
    block = pl.BlockSpec((rows, 2 * HEAD), side)
    out_shape = [
        jax.ShapeDtypeStruct((rows, both // 2), jnp.float32),
        jax.ShapeDtypeStruct((rows, both // 2), jnp.bfloat16),
    ]
    out_specs = [pl.BlockSpec((rows, HEAD), side)] * 2
    in_specs = [pl.BlockSpec((rows, width), fixed)] * (len(whole) + len(part))
    scratch = []
    if part:
        out_shape.append(jax.ShapeDtypeStruct((rows, both), jnp.float32))
        out_specs.append(block)
    if so_far is None:
        split = [len(g) for g in (whole, part) if g]
        body, more = functools.partial(project_body, split), []
        in_specs.append(pl.BlockSpec((depth, 2 * HEAD), side))
        scratch = [pltpu.VMEM((rows, depth), jnp.bfloat16)] * len(split)
    else:
        body, more = project_last_body, [so_far]
        in_specs += [pl.BlockSpec((width, 2 * HEAD), lambda j, info: (info[0], j)), block]
    return pl.pallas_call(
        body,
        out_shape=out_shape,
        grid_spec=pltpu.PrefetchScalarGridSpec(
            num_scalar_prefetch=1,
            grid=(both // (2 * HEAD),),
            in_specs=in_specs,
            out_specs=out_specs,
            scratch_shapes=scratch,
        ),
        compiler_params=pltpu.CompilerParams(vmem_limit_bytes=VMEM),
        cost_estimate=FREE,
    )(order, *whole, *part, weight, *more)


def finish_body(total, info, *refs):
    bias_ref, out_ref = refs[2 * total], refs[-1]
    for i in range(total):

        @pl.when(pl.program_id(0) == i)
        def _():
            value = refs[2 * i][...] + refs[2 * i + 1][...].astype(jnp.float32) + bias_ref[...]
            out_ref[...] = jnp.where(info[total + i] == 1, value, 0.0).astype(jnp.bfloat16)


def finish(info, parts, bias, out):
    rows, columns = parts[0].shape
    total = len(parts) // 2
    whole = pl.BlockSpec((rows, columns), lambda j, info: (0, 0))
    extra = [] if out is None else [out]
    return pl.pallas_call(
        functools.partial(finish_body, total),
        out_shape=jax.ShapeDtypeStruct((3 * rows, columns), jnp.bfloat16),
        grid_spec=pltpu.PrefetchScalarGridSpec(
            num_scalar_prefetch=1,
            grid=(total,),
            in_specs=[whole] * len(parts)
            + [pl.BlockSpec((1, columns), lambda j, info: (0, 0))]
            + [pl.BlockSpec(memory_space=pl.ANY)] * len(extra),
            out_specs=pl.BlockSpec((rows, columns), lambda j, info: (info[j], 0)),
        ),
        input_output_aliases={2 + len(parts): 0} if extra else {},
        compiler_params=pltpu.CompilerParams(vmem_limit_bytes=VMEM),
        cost_estimate=FREE,
    )(info, *parts, bias.reshape(1, columns), *extra)


def pack_body(info, k0_ref, v0_ref, k1_ref, v1_ref, near_ref, key_ref, value_ref):
    near_ref[:FRAME, :] = k0_ref[...]
    near_ref[FRAME:, :] = v0_ref[...]
    key_ref[...] = k1_ref[...]
    value_ref[...] = v1_ref[...]


def pack(info, key, value):
    width = key.shape[1]
    frames = [pl.BlockSpec((FRAME, width), lambda i, info, c=c: (info[c], 0)) for c in (0, 0, 1, 1)]
    heights = (2 * FRAME, FRAME, FRAME)
    return pl.pallas_call(
        pack_body,
        out_shape=[jax.ShapeDtypeStruct((rows, width), key.dtype) for rows in heights],
        grid_spec=pltpu.PrefetchScalarGridSpec(
            num_scalar_prefetch=1,
            grid=(1,),
            in_specs=frames,
            out_specs=[pl.BlockSpec((rows, width), lambda i, info: (0, 0)) for rows in heights],
        ),
        compiler_params=pltpu.CompilerParams(vmem_limit_bytes=60 * 1024 * 1024),
        cost_estimate=FREE,
    )(info, key, value, key, value)


def lay_body(home, own_ref, over_ref, beside_ref, *rest):
    out_ref = rest[-1]
    for j in range(own_ref.shape[1] // HEAD):
        columns = slice(j * HEAD, (j + 1) * HEAD)
        mine = jnp.where(home[0] == 1, own_ref[:, columns], over_ref[:, columns])
        out_ref[:, 2 * j * HEAD : (2 * j + 1) * HEAD] = mine
        out_ref[:, (2 * j + 1) * HEAD : (2 * j + 2) * HEAD] = beside_ref[:, columns]


def lay(home, own, over, beside, after):
    rows, columns = own.shape
    vmem = pl.BlockSpec(memory_space=pltpu.VMEM)
    return pl.pallas_call(
        lay_body,
        out_shape=jax.ShapeDtypeStruct((rows, 2 * columns), own.dtype),
        in_specs=[pl.BlockSpec(memory_space=pltpu.SMEM)]
        + [vmem] * 3
        + [pl.BlockSpec(memory_space=pl.ANY)] * len(after),
        out_specs=vmem,
        cost_estimate=FREE,
    )(home, own, over, beside, *after)


def on_device(query, key, value, slab_counts, out_weight, out_bias):
    count = slab_counts[0]
    x, zh, zl, core = (lax.axis_index(name) for name in ("x", "zh", "zl", "core"))
    seq = lax.axis_index(SEQ)
    seq_width, row = lax.axis_size(SEQ), lax.axis_size("x")
    even = x % 2 == 0
    last = count - 1

    near_slot = jnp.where(even, last, 0)
    away_slot = jnp.where(even, 0, last)
    near_pack, away_key, away_value = pack(jnp.stack([near_slot, away_slot]), key, value)
    near = lax.ppermute(near_pack, "x", [(0, 1), (1, 0), (2, 3), (3, 2)])
    key_round = lax.ppermute(away_key, "x", [(0, 3), (3, 0), (1, 2), (2, 1)])
    value_side = lax.ppermute(away_value, "x", [(0, 1), (3, 2)])
    value_inner = lax.ppermute(away_value, "x", [(1, 2), (2, 1)])

    def across_rows(value, up, down):
        rows = range(seq_width // row - 1)
        pairs = [(r * row + up, (r + 1) * row + up) for r in rows]
        pairs += [((r + 1) * row + down, r * row + down) for r in rows]
        return lax.ppermute(value, SEQ, pairs)

    key_far = across_rows(key_round, 0, 3)
    value_far = lax.ppermute(across_rows(value_side, 2, 1), "x", [(2, 0), (1, 3)])
    near_halo = [(near, 0), (near, 1)]
    inner_halo = [(key_round, 0), (value_inner, 0)]
    far_halo = [(key_far, 0), (value_far, 0)]

    slots = [
        jnp.where(count == 3, 1, jnp.where(count == 2, 2, 1)),
        jnp.where(count == 1, 2, near_slot),
        jnp.where(count == 1, 0, away_slot),
    ]
    actives = [count == 3, count >= 2, count >= 1]
    away_from = jnp.where((x == 1) | (x == 2), 4, 5)

    def frame(c, halos, after):
        slot = slots[c]
        prev_from = jnp.where(slot > 0, slot - 1, jnp.where(even, away_from, 3))
        next_from = jnp.where(slot < last, slot + 1, jnp.where(even, 3, away_from))
        prev_ok = (slot > 0) | (seq > 0)
        next_ok = (slot < last) | (seq < seq_width - 1)
        info = jnp.stack(
            [v.astype(jnp.int32) for v in (slot, prev_from, next_from, prev_ok, next_ok, actives[c])]
        )
        return attend(info, query, key, value, halos, after)

    lines = lax.axis_size("zl")

    def along(value, steps):
        return lax.ppermute(value, "zl", [(i, (i + steps) % lines) for i in range(lines)])

    a = frame(0, [], [])
    a1, a3 = along(a, 1), along(a, -1)
    b = frame(1, near_halo, [])
    b1, b3 = along(b, 1), along(b, -1)
    c = frame(2, near_halo + inner_halo + far_halo, [a1, a3, b1, b3])
    a2, b2 = along(a1, 1), along(b1, 1)
    c1, c3 = along(c, 1), along(c, -1)
    c2 = along(c1, 1)

    home = zh == core
    over = lax.ppermute(out_weight, "zh", [(0, 1), (1, 0)])
    beside = lax.ppermute(jnp.where(home, over, out_weight), "core", [(0, 1), (1, 0)])
    laid = lay(home.astype(jnp.int32).reshape(1), out_weight, over, beside, [key_round, value_side, near, a1])
    weight = lax.all_gather(laid, ("y", "x"), axis=0, tiled=True)

    order = [((zl - k) % lines).astype(jnp.int32) for k in range(lines)]

    def swap(value):
        return lax.ppermute(value, "core", [(0, 1), (1, 0)])

    def put(indices, parts, out):
        info = jnp.stack([v[i].astype(jnp.int32) for v in (slots, actives) for i in indices])
        return finish(info, parts, out_bias, out)

    own_a, other_a = project(jnp.stack(order), [a, a1, a2, a3], [], weight)
    out = put([0], [own_a, swap(other_a)], None)
    turns = jnp.stack(order + [order[0], order[1], order[3]])
    own_b, other_b, so_far = project(turns, [b, b1, b2, b3], [c, c1, c3], weight)
    own_c, other_c = project(order[2].reshape(1), [c2], [], weight, so_far)
    out = put([1, 2], [own_b, swap(other_b), own_c, swap(other_c)], out)
    return out.T


def solution(mesh):
    fine = Mesh(mesh.devices.reshape(4, 2, 4, 2, 4), FSDP + SEQ)
    tiles = P(SEQ, FSDP)
    return jax.shard_map(
        on_device,
        mesh=fine,
        in_specs=(tiles, tiles, tiles, P(SEQ), tiles, P(FSDP)),
        out_specs=P(FSDP, SEQ),
        check_vma=False,
    )
```

```python
import functools

import jax
import jax.numpy as jnp
from jax import lax
from jax.experimental import pallas as pl
from jax.experimental.pallas import tpu as pltpu
from jax.sharding import Mesh
from jax.sharding import PartitionSpec as P

HEAD = 128
TILE = 192
FRAME = 576
LN2 = 0.6931471805599453
SCALE = HEAD**-0.5 / LN2
FAR = 1e30
SEQ = ("y", "zh", "x")
FSDP = ("zl", "core")
VMEM = 48 * 1024 * 1024
FREE = pl.CostEstimate(flops=0, bytes_accessed=0, transcendentals=0)


def attend_body(halo_total, info, q_ref, k_ref, v_ref, *rest):
    halos, (o_ref, kbuf, vbuf) = rest[:halo_total], rest[-3:]
    slot, prev_from, next_from, prev_ok, next_ok, active = (info[i] for i in range(6))

    @pl.when(active == 0)
    def _():
        o_ref[...] = jnp.zeros_like(o_ref)

    def fill(place, source):
        rows = pl.ds(place * FRAME, FRAME)

        @pl.when(source < 3)
        def _():
            local = pl.ds(pl.multiple_of(jnp.clip(source, 0, 2) * FRAME, FRAME), FRAME)
            kbuf[rows, :] = k_ref[local, :]
            vbuf[rows, :] = v_ref[local, :]

        for i in range(halo_total // 2):

            @pl.when(source == 3 + i)
            def _():
                kbuf[rows, :] = halos[2 * i][...]
                vbuf[rows, :] = halos[2 * i + 1][...]

    @pl.when(active == 1)
    def _():
        fill(0, prev_from)
        fill(1, slot)
        fill(2, next_from)
        off = [jnp.where(prev_ok == 1, 0.0, FAR), jnp.float32(0.0), jnp.where(next_ok == 1, 0.0, FAR)]
        for w in range(3):
            low, high = max(0, w - 1) * TILE, min(3, w + 2) * TILE
            q = q_ref[pl.ds(pl.multiple_of(slot * FRAME + w * TILE, TILE), TILE), :]
            scores, tops = [], []
            for f in range(3):
                keys = kbuf[f * FRAME + low : f * FRAME + high, :]
                s = lax.dot_general(q, keys, (((1,), (1,)), ((), ())), preferred_element_type=jnp.float32)
                scores.append(s)
                tops.append(jnp.max(s, axis=1, keepdims=True) * SCALE - off[f])
            top = jnp.maximum(jnp.maximum(tops[0], tops[1]), tops[2])
            total, mass = None, None
            for f in range(3):
                p = jnp.exp2(scores[f] * SCALE - (top + off[f]))
                values = vbuf[f * FRAME + low : f * FRAME + high, :]
                part = jnp.dot(p.astype(jnp.bfloat16), values, preferred_element_type=jnp.float32)
                row = jnp.sum(p, axis=1, keepdims=True)
                total, mass = (part, row) if total is None else (total + part, mass + row)
            o_ref[w * TILE : (w + 1) * TILE, :] = (total / mass).astype(jnp.bfloat16)


def attend(info, query, key, value, halos, after):
    rows, width = query.shape
    heads = width // HEAD
    column = lambda h, info: (0, h)
    whole = pl.BlockSpec((rows, HEAD), column)
    one = pl.BlockSpec((FRAME, HEAD), column)
    where = [pl.BlockSpec((FRAME, HEAD), lambda h, info, r=r: (r, h)) for _, r in halos]
    return pl.pallas_call(
        functools.partial(attend_body, len(halos)),
        out_shape=jax.ShapeDtypeStruct((FRAME, width), jnp.bfloat16),
        grid_spec=pltpu.PrefetchScalarGridSpec(
            num_scalar_prefetch=1,
            grid=(heads,),
            in_specs=[whole] * 3 + where + [pl.BlockSpec(memory_space=pl.ANY)] * len(after),
            out_specs=one,
            scratch_shapes=[
                pltpu.VMEM((3 * FRAME, HEAD), jnp.bfloat16),
                pltpu.VMEM((3 * FRAME, HEAD), jnp.bfloat16),
            ],
        ),
        compiler_params=pltpu.CompilerParams(vmem_limit_bytes=VMEM),
        cost_estimate=FREE,
    )(info, query, key, value, *[array for array, _ in halos], *after)


def line_up(info, at, pieces, line):
    width = pieces[0].shape[1]
    if len(pieces) * width < line.shape[1]:
        line[...] = jnp.zeros_like(line)
    for k, piece in enumerate(pieces):
        line[:, pl.ds(pl.multiple_of(info[at + k] * width, width), width)] = piece[...]


def project_body(split, info, *refs):
    total = sum(split)
    pieces, w_ref = refs[:total], refs[total]
    mine_ref, other_ref, line = refs[-3:]
    rows, columns = line.shape[0], mine_ref.shape[1]
    at = 0
    for c, size in enumerate(split):
        line_up(info, at, pieces[at : at + size], line)
        at += size
        share = jnp.dot(line[...], w_ref[...], preferred_element_type=jnp.float32)
        mine_ref[c * rows : (c + 1) * rows, :] = share[:, :columns].astype(mine_ref.dtype)
        other_ref[c * rows : (c + 1) * rows, :] = share[:, columns:].astype(other_ref.dtype)


def project_last_body(info, piece, w_ref, mine_far, other_far, mine_ref, other_ref):
    columns = mine_ref.shape[1]
    total = jnp.dot(piece[...], w_ref[...], preferred_element_type=jnp.float32)
    mine_ref[...] = total[:, :columns] + mine_far[...]
    other_ref[...] = (total[:, columns:] + other_far[...]).astype(other_ref.dtype)


def project(order, chunks, weight, dtypes, after=()):
    rows, width = chunks[0][0].shape
    depth, both = weight.shape
    fixed = lambda j, info: (0, 0)
    pieces = [piece for chunk in chunks for piece in chunk]
    tall = (len(chunks) * rows, both // 2)
    return pl.pallas_call(
        functools.partial(project_body, [len(chunk) for chunk in chunks]),
        out_shape=[jax.ShapeDtypeStruct(tall, dtype) for dtype in dtypes],
        grid_spec=pltpu.PrefetchScalarGridSpec(
            num_scalar_prefetch=1,
            grid=(1,),
            in_specs=[pl.BlockSpec((rows, width), fixed)] * len(pieces)
            + [pl.BlockSpec((depth, both), fixed)]
            + [pl.BlockSpec(memory_space=pl.ANY)] * len(after),
            out_specs=[pl.BlockSpec(tall, fixed)] * 2,
            scratch_shapes=[pltpu.VMEM((rows, depth), jnp.bfloat16)],
        ),
        compiler_params=pltpu.CompilerParams(vmem_limit_bytes=VMEM),
        cost_estimate=FREE,
    )(order, *pieces, weight, *after)


def project_last(order, piece, weight, mine_far, other_far):
    rows, width = piece.shape
    both = weight.shape[1]
    fixed = lambda j, info: (0, 0)
    out = pl.BlockSpec((rows, both // 2), fixed)
    return pl.pallas_call(
        project_last_body,
        out_shape=[jax.ShapeDtypeStruct((rows, both // 2), dtype) for dtype in (jnp.float32, jnp.bfloat16)],
        grid_spec=pltpu.PrefetchScalarGridSpec(
            num_scalar_prefetch=1,
            grid=(1,),
            in_specs=[
                pl.BlockSpec((rows, width), fixed),
                pl.BlockSpec((width, both), lambda j, info: (info[0], 0)),
                out,
                out,
            ],
            out_specs=[out] * 2,
        ),
        compiler_params=pltpu.CompilerParams(vmem_limit_bytes=VMEM),
        cost_estimate=FREE,
    )(order, piece, weight, mine_far, other_far)


def finish_body(total, info, mine_ref, received_ref, bias_ref, *rest):
    value = mine_ref[...] + received_ref[...].astype(jnp.float32) + bias_ref[...]
    active = info[total + pl.program_id(0)]
    rest[-1][...] = jnp.where(active == 1, value, 0.0).astype(jnp.bfloat16)


def finish(info, mine, received, bias, out):
    rows, columns = mine.shape
    total = rows // FRAME
    block = pl.BlockSpec((FRAME, columns), lambda j, info: (j, 0))
    extra = [] if out is None else [out]
    return pl.pallas_call(
        functools.partial(finish_body, total),
        out_shape=jax.ShapeDtypeStruct((3 * FRAME, columns), jnp.bfloat16),
        grid_spec=pltpu.PrefetchScalarGridSpec(
            num_scalar_prefetch=1,
            grid=(total,),
            in_specs=[block, block, pl.BlockSpec((1, columns), lambda j, info: (0, 0))]
            + [pl.BlockSpec(memory_space=pl.ANY)] * len(extra),
            out_specs=pl.BlockSpec((FRAME, columns), lambda j, info: (info[j], 0)),
        ),
        input_output_aliases={4: 0} if extra else {},
        compiler_params=pltpu.CompilerParams(vmem_limit_bytes=VMEM),
        cost_estimate=FREE,
    )(info, mine, received, bias.reshape(1, columns), *extra)


def pack_body(info, k0_ref, v0_ref, k1_ref, v1_ref, *rest):
    near_ref, key_ref, value_ref = rest[-3:]
    near_ref[:FRAME, :] = k0_ref[...]
    near_ref[FRAME:, :] = v0_ref[...]
    key_ref[...] = k1_ref[...]
    value_ref[...] = v1_ref[...]


def pack(info, key, value, after):
    width = key.shape[1]
    frames = [pl.BlockSpec((FRAME, width), lambda i, info, c=c: (info[c], 0)) for c in (0, 0, 1, 1)]
    heights = (2 * FRAME, FRAME, FRAME)
    return pl.pallas_call(
        pack_body,
        out_shape=[jax.ShapeDtypeStruct((rows, width), key.dtype) for rows in heights],
        grid_spec=pltpu.PrefetchScalarGridSpec(
            num_scalar_prefetch=1,
            grid=(1,),
            in_specs=frames + [pl.BlockSpec(memory_space=pl.ANY)] * len(after),
            out_specs=[pl.BlockSpec((rows, width), lambda i, info: (0, 0)) for rows in heights],
        ),
        compiler_params=pltpu.CompilerParams(vmem_limit_bytes=60 * 1024 * 1024),
        cost_estimate=FREE,
    )(info, key, value, key, value, *after)


def lay_body(home, own_ref, over_ref, beside_ref, *rest):
    out_ref = rest[-1]
    columns = own_ref.shape[1]
    out_ref[:, :columns] = jnp.where(home[0] == 1, own_ref[...], over_ref[...])
    out_ref[:, columns:] = beside_ref[...]


def lay(home, own, over, beside, after):
    rows, columns = own.shape
    vmem = pl.BlockSpec(memory_space=pltpu.VMEM)
    return pl.pallas_call(
        lay_body,
        out_shape=jax.ShapeDtypeStruct((rows, 2 * columns), own.dtype),
        in_specs=[pl.BlockSpec(memory_space=pltpu.SMEM)]
        + [vmem] * 3
        + [pl.BlockSpec(memory_space=pl.ANY)] * len(after),
        out_specs=vmem,
        cost_estimate=FREE,
    )(home, own, over, beside, *after)


def on_device(query, key, value, slab_counts, out_weight, out_bias):
    count = slab_counts[0]
    x, y, zh, zl, core = (lax.axis_index(name) for name in ("x", "y", "zh", "zl", "core"))
    seq = lax.axis_index(SEQ)
    seq_width, row = lax.axis_size(SEQ), lax.axis_size("x")
    even = x % 2 == 0
    last = count - 1

    near_slot = jnp.where(even, last, 0)
    away_slot = jnp.where(even, 0, last)

    slots = [
        jnp.where(count == 3, 1, jnp.where(count == 2, 2, 1)),
        jnp.where(count == 1, 2, near_slot),
        jnp.where(count == 1, 0, away_slot),
    ]
    actives = [count == 3, count >= 2, count >= 1]
    away_from = jnp.where((x == 1) | (x == 2), 4, 5)

    def frame(c, halos, after):
        slot = slots[c]
        prev_from = jnp.where(slot > 0, slot - 1, jnp.where(even, away_from, 3))
        next_from = jnp.where(slot < last, slot + 1, jnp.where(even, 3, away_from))
        prev_ok = (slot > 0) | (seq > 0)
        next_ok = (slot < last) | (seq < seq_width - 1)
        info = jnp.stack(
            [v.astype(jnp.int32) for v in (slot, prev_from, next_from, prev_ok, next_ok, actives[c])]
        )
        return attend(info, query, key, value, halos, after)

    lines = lax.axis_size("zl")

    def along(value, steps):
        return lax.ppermute(value, "zl", [(i, (i + steps) % lines) for i in range(lines)])

    a = frame(0, [], [])
    a1, a3 = along(a, 1), along(a, -1)
    near_pack, away_key, away_value = pack(jnp.stack([near_slot, away_slot]), key, value, [])
    near = lax.ppermute(near_pack, "x", [(0, 1), (1, 0), (2, 3), (3, 2)])
    key_round = lax.ppermute(away_key, "x", [(0, 3), (3, 0), (1, 2), (2, 1)])
    value_side = lax.ppermute(away_value, "x", [(0, 1), (3, 2)])
    value_inner = lax.ppermute(away_value, "x", [(1, 2), (2, 1)])

    def across_rows(value, up, down):
        rows = range(seq_width // row - 1)
        pairs = [(r * row + up, (r + 1) * row + up) for r in rows]
        pairs += [((r + 1) * row + down, r * row + down) for r in rows]
        return lax.ppermute(value, SEQ, pairs)

    key_far = across_rows(key_round, 0, 3)
    value_mid = across_rows(value_side, 2, 1)
    value_far = lax.ppermute(value_mid, "x", [(2, 0), (1, 3)])
    near_halo = [(near, 0), (near, 1)]
    inner_halo = [(key_round, 0), (value_inner, 0)]
    far_halo = [(key_far, 0), (value_far, 0)]

    b = frame(1, near_halo, [])
    b1, b3 = along(b, 1), along(b, -1)
    a2, b2 = along(a1, 1), along(b1, 1)
    home = zh == core
    over = lax.ppermute(out_weight, "zh", [(0, 1), (1, 0)])
    beside = lax.ppermute(jnp.where(home, over, out_weight), "core", [(0, 1), (1, 0)])
    laid = lay(home.astype(jnp.int32).reshape(1), out_weight, over, beside, [key_round, value_side, a])
    weight = lax.all_gather(laid, ("y", "x"), axis=0, tiled=True)

    c = frame(2, near_halo + inner_halo + far_halo, [b1])
    c1, c3 = along(c, 1), along(c, -1)
    c2 = along(c1, 1)

    order = [((zl - k) % lines).astype(jnp.int32) for k in range(lines)]

    def swap(value):
        return lax.ppermute(value, "core", [(0, 1), (1, 0)])

    def put(indices, mine, received, out):
        info = jnp.stack([v[i].astype(jnp.int32) for v in (slots, actives) for i in indices])
        return finish(info, mine, received, out_bias, out)

    types = (jnp.float32, jnp.bfloat16)
    own_a, other_a = project(jnp.stack(order), [[a, a1, a2, a3]], weight, types, [])
    own_b, other_b = project(jnp.stack(order), [[b, b1, b2, b3]], weight, types)
    so_far = project(
        jnp.stack([order[0], order[1], order[3]]), [[c, c1, c3]], weight, (jnp.bfloat16, jnp.bfloat16)
    )
    own_c, other_c = project_last(order[2].reshape(1), c2, weight, *so_far)
    out = put([0], own_a, swap(other_a), None)
    out = put([1], own_b, swap(other_b), out)
    out = put([2], own_c, swap(other_c), out)
    return out.T


def solution(mesh):
    fine = Mesh(mesh.devices.reshape(4, 2, 4, 2, 4), FSDP + SEQ)
    tiles = P(SEQ, FSDP)
    return jax.shard_map(
        on_device,
        mesh=fine,
        in_specs=(tiles, tiles, tiles, P(SEQ), tiles, P(FSDP)),
        out_specs=P(FSDP, SEQ),
        check_vma=False,
    )
```

```python
import functools

import jax
import jax.numpy as jnp
from jax import lax
from jax.experimental import pallas as pl
from jax.experimental.pallas import tpu as pltpu
from jax.sharding import Mesh
from jax.sharding import PartitionSpec as P

HEAD = 128
TILE = 192
FRAME = 576
LN2 = 0.6931471805599453
SCALE = HEAD**-0.5 / LN2
FAR = 1e30
SEQ = ("y", "zh", "x")
FSDP = ("zl", "core")
VMEM = 48 * 1024 * 1024
FREE = pl.CostEstimate(flops=0, bytes_accessed=0, transcendentals=0)


def attend_body(halo_total, info, q_ref, k_ref, v_ref, *rest):
    halos, (o_ref, kbuf, vbuf) = rest[:halo_total], rest[-3:]
    slot, prev_from, next_from, prev_ok, next_ok, active = (info[i] for i in range(6))

    @pl.when(active == 0)
    def _():
        o_ref[...] = jnp.zeros_like(o_ref)

    def fill(place, source):
        rows = pl.ds(place * FRAME, FRAME)

        @pl.when(source < 3)
        def _():
            local = pl.ds(pl.multiple_of(jnp.clip(source, 0, 2) * FRAME, FRAME), FRAME)
            kbuf[rows, :] = k_ref[local, :]
            vbuf[rows, :] = v_ref[local, :]

        for i in range(halo_total // 2):

            @pl.when(source == 3 + i)
            def _():
                kbuf[rows, :] = halos[2 * i][...]
                vbuf[rows, :] = halos[2 * i + 1][...]

    @pl.when(active == 1)
    def _():
        fill(0, prev_from)
        fill(1, slot)
        fill(2, next_from)
        off = [jnp.where(prev_ok == 1, 0.0, FAR), jnp.float32(0.0), jnp.where(next_ok == 1, 0.0, FAR)]
        for w in range(3):
            low, high = max(0, w - 1) * TILE, min(3, w + 2) * TILE
            q = q_ref[pl.ds(pl.multiple_of(slot * FRAME + w * TILE, TILE), TILE), :]
            scores, tops = [], []
            for f in range(3):
                keys = kbuf[f * FRAME + low : f * FRAME + high, :]
                s = lax.dot_general(q, keys, (((1,), (1,)), ((), ())), preferred_element_type=jnp.float32)
                scores.append(s)
                tops.append(jnp.max(s, axis=1, keepdims=True) * SCALE - off[f])
            top = jnp.maximum(jnp.maximum(tops[0], tops[1]), tops[2])
            total, mass = None, None
            for f in range(3):
                p = jnp.exp2(scores[f] * SCALE - (top + off[f]))
                values = vbuf[f * FRAME + low : f * FRAME + high, :]
                part = jnp.dot(p.astype(jnp.bfloat16), values, preferred_element_type=jnp.float32)
                row = jnp.sum(p, axis=1, keepdims=True)
                total, mass = (part, row) if total is None else (total + part, mass + row)
            o_ref[w * TILE : (w + 1) * TILE, :] = (total / mass).astype(jnp.bfloat16)


def attend(info, query, key, value, halos, after):
    rows, width = query.shape
    heads = width // HEAD
    column = lambda h, info: (0, h)
    whole = pl.BlockSpec((rows, HEAD), column)
    one = pl.BlockSpec((FRAME, HEAD), column)
    where = [pl.BlockSpec((FRAME, HEAD), lambda h, info, r=r: (r, h)) for _, r in halos]
    return pl.pallas_call(
        functools.partial(attend_body, len(halos)),
        out_shape=jax.ShapeDtypeStruct((FRAME, width), jnp.bfloat16),
        grid_spec=pltpu.PrefetchScalarGridSpec(
            num_scalar_prefetch=1,
            grid=(heads,),
            in_specs=[whole] * 3 + where + [pl.BlockSpec(memory_space=pl.ANY)] * len(after),
            out_specs=one,
            scratch_shapes=[
                pltpu.VMEM((3 * FRAME, HEAD), jnp.bfloat16),
                pltpu.VMEM((3 * FRAME, HEAD), jnp.bfloat16),
            ],
        ),
        compiler_params=pltpu.CompilerParams(vmem_limit_bytes=VMEM),
        cost_estimate=FREE,
    )(info, query, key, value, *[array for array, _ in halos], *after)


def line_up(info, at, pieces, line):
    width = pieces[0].shape[1]
    if len(pieces) * width < line.shape[1]:
        line[...] = jnp.zeros_like(line)
    for k, piece in enumerate(pieces):
        line[:, pl.ds(pl.multiple_of(info[at + k] * width, width), width)] = piece[...]


def project_body(split, info, *refs):
    total = sum(split)
    pieces, w_ref = refs[:total], refs[total]
    mine_ref, other_ref, line = refs[-3:]
    rows, columns = line.shape[0], mine_ref.shape[1]
    at = 0
    for c, size in enumerate(split):
        line_up(info, at, pieces[at : at + size], line)
        at += size
        share = jnp.dot(line[...], w_ref[...], preferred_element_type=jnp.float32)
        mine_ref[c * rows : (c + 1) * rows, :] = share[:, :columns].astype(mine_ref.dtype)
        other_ref[c * rows : (c + 1) * rows, :] = share[:, columns:].astype(other_ref.dtype)


def project_last_body(info, piece, w_ref, mine_far, other_far, mine_ref, other_ref):
    columns = mine_ref.shape[1]
    total = jnp.dot(piece[...], w_ref[...], preferred_element_type=jnp.float32)
    mine_ref[...] = total[:, :columns] + mine_far[...]
    other_ref[...] = (total[:, columns:] + other_far[...]).astype(other_ref.dtype)


def project(order, chunks, weight, dtypes, after=()):
    rows, width = chunks[0][0].shape
    depth, both = weight.shape
    fixed = lambda j, info: (0, 0)
    pieces = [piece for chunk in chunks for piece in chunk]
    tall = (len(chunks) * rows, both // 2)
    return pl.pallas_call(
        functools.partial(project_body, [len(chunk) for chunk in chunks]),
        out_shape=[jax.ShapeDtypeStruct(tall, dtype) for dtype in dtypes],
        grid_spec=pltpu.PrefetchScalarGridSpec(
            num_scalar_prefetch=1,
            grid=(1,),
            in_specs=[pl.BlockSpec((rows, width), fixed)] * len(pieces)
            + [pl.BlockSpec((depth, both), fixed)]
            + [pl.BlockSpec(memory_space=pl.ANY)] * len(after),
            out_specs=[pl.BlockSpec(tall, fixed)] * 2,
            scratch_shapes=[pltpu.VMEM((rows, depth), jnp.bfloat16)],
        ),
        compiler_params=pltpu.CompilerParams(vmem_limit_bytes=VMEM),
        cost_estimate=FREE,
    )(order, *pieces, weight, *after)


def project_last(order, piece, weight, mine_far, other_far):
    rows, width = piece.shape
    both = weight.shape[1]
    fixed = lambda j, info: (0, 0)
    out = pl.BlockSpec((rows, both // 2), fixed)
    return pl.pallas_call(
        project_last_body,
        out_shape=[jax.ShapeDtypeStruct((rows, both // 2), dtype) for dtype in (jnp.float32, jnp.bfloat16)],
        grid_spec=pltpu.PrefetchScalarGridSpec(
            num_scalar_prefetch=1,
            grid=(1,),
            in_specs=[
                pl.BlockSpec((rows, width), fixed),
                pl.BlockSpec((width, both), lambda j, info: (info[0], 0)),
                out,
                out,
            ],
            out_specs=[out] * 2,
        ),
        compiler_params=pltpu.CompilerParams(vmem_limit_bytes=VMEM),
        cost_estimate=FREE,
    )(order, piece, weight, mine_far, other_far)


def finish_body(total, info, mine_ref, received_ref, bias_ref, *rest):
    value = mine_ref[...] + received_ref[...].astype(jnp.float32) + bias_ref[...]
    active = info[total + pl.program_id(0)]
    rest[-1][...] = jnp.where(active == 1, value, 0.0).astype(jnp.bfloat16)


def finish(info, mine, received, bias, out):
    rows, columns = mine.shape
    total = rows // FRAME
    block = pl.BlockSpec((FRAME, columns), lambda j, info: (j, 0))
    extra = [] if out is None else [out]
    return pl.pallas_call(
        functools.partial(finish_body, total),
        out_shape=jax.ShapeDtypeStruct((3 * FRAME, columns), jnp.bfloat16),
        grid_spec=pltpu.PrefetchScalarGridSpec(
            num_scalar_prefetch=1,
            grid=(total,),
            in_specs=[block, block, pl.BlockSpec((1, columns), lambda j, info: (0, 0))]
            + [pl.BlockSpec(memory_space=pl.ANY)] * len(extra),
            out_specs=pl.BlockSpec((FRAME, columns), lambda j, info: (info[j], 0)),
        ),
        input_output_aliases={4: 0} if extra else {},
        compiler_params=pltpu.CompilerParams(vmem_limit_bytes=VMEM),
        cost_estimate=FREE,
    )(info, mine, received, bias.reshape(1, columns), *extra)


def pack_body(info, k0_ref, v0_ref, k1_ref, v1_ref, *rest):
    near_ref, key_ref, value_ref = rest[-3:]
    near_ref[:FRAME, :] = k0_ref[...]
    near_ref[FRAME:, :] = v0_ref[...]
    key_ref[...] = k1_ref[...]
    value_ref[...] = v1_ref[...]


def pack(info, key, value, after):
    width = key.shape[1]
    frames = [pl.BlockSpec((FRAME, width), lambda i, info, c=c: (info[c], 0)) for c in (0, 0, 1, 1)]
    heights = (2 * FRAME, FRAME, FRAME)
    return pl.pallas_call(
        pack_body,
        out_shape=[jax.ShapeDtypeStruct((rows, width), key.dtype) for rows in heights],
        grid_spec=pltpu.PrefetchScalarGridSpec(
            num_scalar_prefetch=1,
            grid=(1,),
            in_specs=frames + [pl.BlockSpec(memory_space=pl.ANY)] * len(after),
            out_specs=[pl.BlockSpec((rows, width), lambda i, info: (0, 0)) for rows in heights],
        ),
        compiler_params=pltpu.CompilerParams(vmem_limit_bytes=60 * 1024 * 1024),
        cost_estimate=FREE,
    )(info, key, value, key, value, *after)


def lay_body(home, own_ref, over_ref, beside_ref, *rest):
    out_ref = rest[-1]
    columns = own_ref.shape[1]
    out_ref[:, :columns] = jnp.where(home[0] == 1, own_ref[...], over_ref[...])
    out_ref[:, columns:] = beside_ref[...]


def lay(home, own, over, beside, after):
    rows, columns = own.shape
    vmem = pl.BlockSpec(memory_space=pltpu.VMEM)
    return pl.pallas_call(
        lay_body,
        out_shape=jax.ShapeDtypeStruct((rows, 2 * columns), own.dtype),
        in_specs=[pl.BlockSpec(memory_space=pltpu.SMEM)]
        + [vmem] * 3
        + [pl.BlockSpec(memory_space=pl.ANY)] * len(after),
        out_specs=vmem,
        cost_estimate=FREE,
    )(home, own, over, beside, *after)


def on_device(query, key, value, slab_counts, out_weight, out_bias):
    count = slab_counts[0]
    x, y, zh, zl, core = (lax.axis_index(name) for name in ("x", "y", "zh", "zl", "core"))
    seq = lax.axis_index(SEQ)
    seq_width, row = lax.axis_size(SEQ), lax.axis_size("x")
    even = x % 2 == 0
    last = count - 1

    near_slot = jnp.where(even, last, 0)
    away_slot = jnp.where(even, 0, last)

    slots = [
        jnp.where(count == 3, 1, jnp.where(count == 2, 2, 1)),
        jnp.where(count == 1, 2, near_slot),
        jnp.where(count == 1, 0, away_slot),
    ]
    actives = [count == 3, count >= 2, count >= 1]
    away_from = jnp.where((x == 1) | (x == 2), 4, 5)

    def frame(c, halos, after):
        slot = slots[c]
        prev_from = jnp.where(slot > 0, slot - 1, jnp.where(even, away_from, 3))
        next_from = jnp.where(slot < last, slot + 1, jnp.where(even, 3, away_from))
        prev_ok = (slot > 0) | (seq > 0)
        next_ok = (slot < last) | (seq < seq_width - 1)
        info = jnp.stack(
            [v.astype(jnp.int32) for v in (slot, prev_from, next_from, prev_ok, next_ok, actives[c])]
        )
        return attend(info, query, key, value, halos, after)

    lines = lax.axis_size("zl")

    def along(value, steps):
        return lax.ppermute(value, "zl", [(i, (i + steps) % lines) for i in range(lines)])

    a = frame(0, [], [])
    a1, a3 = along(a, 1), along(a, -1)
    near_pack, away_key, away_value = pack(jnp.stack([near_slot, away_slot]), key, value, [])
    near = lax.ppermute(near_pack, "x", [(0, 1), (1, 0), (2, 3), (3, 2)])
    key_round = lax.ppermute(away_key, "x", [(0, 3), (3, 0), (1, 2), (2, 1)])
    value_side = lax.ppermute(away_value, "x", [(0, 1), (3, 2)])
    value_inner = lax.ppermute(away_value, "x", [(1, 2), (2, 1)])

    def across_rows(value, up, down):
        rows = range(seq_width // row - 1)
        pairs = [(r * row + up, (r + 1) * row + up) for r in rows]
        pairs += [((r + 1) * row + down, r * row + down) for r in rows]
        return lax.ppermute(value, SEQ, pairs)

    key_far = across_rows(key_round, 0, 3)
    value_mid = across_rows(value_side, 2, 1)
    value_far = lax.ppermute(value_mid, "x", [(2, 0), (1, 3)])
    near_halo = [(near, 0), (near, 1)]
    inner_halo = [(key_round, 0), (value_inner, 0)]
    far_halo = [(key_far, 0), (value_far, 0)]

    b = frame(1, near_halo, [])
    b1, b3 = along(b, 1), along(b, -1)
    a2, b2 = along(a1, 1), along(b1, 1)
    home = zh == core
    over = lax.ppermute(out_weight, "zh", [(0, 1), (1, 0)])
    beside = lax.ppermute(jnp.where(home, over, out_weight), "core", [(0, 1), (1, 0)])
    laid = lay(home.astype(jnp.int32).reshape(1), out_weight, over, beside, [key_round, value_side, a])
    weight = lax.all_gather(laid, ("y", "x"), axis=0, tiled=True)

    c = frame(2, near_halo + inner_halo + far_halo, [])
    c1, c3 = along(c, 1), along(c, -1)
    c2 = along(c1, 1)

    order = [((zl - k) % lines).astype(jnp.int32) for k in range(lines)]

    def swap(value):
        return lax.ppermute(value, "core", [(0, 1), (1, 0)])

    def put(indices, mine, received, out):
        info = jnp.stack([v[i].astype(jnp.int32) for v in (slots, actives) for i in indices])
        return finish(info, mine, received, out_bias, out)

    types = (jnp.float32, jnp.bfloat16)
    own_a, other_a = project(jnp.stack(order), [[a, a1, a2, a3]], weight, types, [])
    own_b, other_b = project(jnp.stack(order), [[b, b1, b2, b3]], weight, types)
    so_far = project(
        jnp.stack([order[0], order[1], order[3]]), [[c, c1, c3]], weight, (jnp.bfloat16, jnp.bfloat16)
    )
    own_c, other_c = project_last(order[2].reshape(1), c2, weight, *so_far)
    out = put([0], own_a, swap(other_a), None)
    out = put([1], own_b, swap(other_b), out)
    out = put([2], own_c, swap(other_c), out)
    return out.T


def solution(mesh):
    fine = Mesh(mesh.devices.reshape(4, 2, 4, 2, 4), FSDP + SEQ)
    tiles = P(SEQ, FSDP)
    return jax.shard_map(
        on_device,
        mesh=fine,
        in_specs=(tiles, tiles, tiles, P(SEQ), tiles, P(FSDP)),
        out_specs=P(FSDP, SEQ),
        check_vma=False,
    )
```
